32 devices in a mesh: ctx: 4 (over y, x), role: 2 (over core), exp: 4 (over z).
Axes of the slice: x: 2, y: 2, z: 4, core: 2. Of those that a mesh axis runs over, the one named last changes fastest.
Arguments:
- queries: bfloat16 [512, 32768], P('ctx', ('role', 'exp')), may hold values from -56 to 56
- latent: bfloat16 [512, 512], P('ctx'), may hold values from -5 to 5
- frames: int32 [512], replicated, may hold values from 0 to 7, never falling along the last dimension, each value on 1 to 128 neighbouring positions
- w_uv: bfloat16 [64, 512, 128], P(('role', 'exp')), may hold values from -0.5 to 0.5
- w_out: bfloat16 [8192, 7168], P(('role', 'exp'), 'ctx'), may hold values from -0.25 to 0.25
- residual: bfloat16 [512, 7168], P('ctx', ('role', 'exp')), may hold values from -40 to 40
- norm_gain: float32 [7168], replicated, may hold values from 0.5 to 2
- expert_ids: int32 [512, 2], P('ctx'), may hold values from 0 to 3, all different within a row; in each aligned block of 128 rows (0 to 127, 128 to 255, ...) at most 80 rows name the same one
- mix_codes: int32 [512, 2], P('ctx'), may hold values from 1 to 256
- w_gate: bfloat16 [4, 7168, 1024], P('ctx', None, ('role', 'exp')), may hold values from -0.0625 to 0.0625
- w_up: bfloat16 [4, 7168, 1024], P('ctx', None, ('role', 'exp')), may hold values from -0.0625 to 0.0625
- w_down: bfloat16 [4, 1024, 7168], P('ctx', ('role', 'exp')), may hold values from -0.375 to 0.375
- grad_out: bfloat16 [512, 7168], P('ctx', ('role', 'exp')), may hold values from -6 to 6
Outputs:
- layer_out: bfloat16 [512, 7168], P('ctx', ('role', 'exp'))
- grad_pre_norm: bfloat16 [512, 7168], P('ctx', ('role', 'exp'))
- grad_gate: bfloat16 [4, 7168, 1024], P('ctx', None, ('role', 'exp'))
- grad_up: bfloat16 [4, 7168, 1024], P('ctx', None, ('role', 'exp'))
- grad_down: bfloat16 [4, 1024, 7168], P('ctx', ('role', 'exp'))
The draws below stay inside these ranges and needn't reach their ends.
Inputs may be any that keep to these rules, and one draw needn't show every extreme that they name: `expert_ids`: each row names 2 different experts. Among the 128 rows of one index of ctx no expert is named more than 80 times, and in some such block one expert is named exactly 80 times. `frames`: never falls along the scene; each frame holds 1 to 128 tokens and one holds exactly 128.
All inputs are finite; a program needn't handle non-finite values.
Results may differ from the reference program's by a relative error of at most 0.03.
Values may be sent and summed in bfloat16 or wider, within the bound.
A program may use at most 128 MiB of HBM per device.

```python
import math
import jax
import jax.numpy as jnp
import numpy as np
from jax import lax

D = 7168
DL = 512
DV = 128
HEADS = 64
FE = 1024
TOPK = 2
TOK_DEV = 128
GROUPS = 8
EXPERTS = 4
SEQ = 512
CAP = 80
FRAMES = 8
N_CTX = 4


def scene_latent(key):
    latent_base = jnp.clip(jax.random.normal(jax.random.fold_in(key, 101), (SEQ, DL), jnp.float32), -4.5, 4.5)
    return latent_base


def draw_latent(key, part):
    latent_base = scene_latent(key)
    return latent_base.astype(jnp.bfloat16)


def draw_queries(key, part):
    query_draw = 1.5 * jnp.clip(jax.random.normal(jax.random.fold_in(key, 201), (SEQ, HEADS * DL), jnp.float32), -4.0, 4.0)
    return query_draw.astype(jnp.bfloat16)


def draw_residual(key, part):
    noise_draw = jnp.clip(jax.random.normal(jax.random.fold_in(key, 301), (SEQ, D), jnp.float32), -4.0, 4.0)
    row_scale = jnp.exp(jax.random.uniform(jax.random.fold_in(key, 302), (SEQ, 1), jnp.float32, math.log(0.25), math.log(2.5)))
    column_rise = math.log(3.0) * jnp.arange(D, dtype=jnp.float32) / (D - 1)
    column_scale = jnp.exp(column_rise[None, :] + jax.random.uniform(jax.random.fold_in(key, 303), (1, D), jnp.float32, -0.22, 0.22))
    return (noise_draw * row_scale * column_scale).astype(jnp.bfloat16)


def plant(array, key, smallest, high):
    longest = array.shape.index(max(array.shape))
    spots = []
    for shift in (0, 1):
        where = [jax.random.randint(jax.random.fold_in(key, axis), (), 0, length) for axis, length in enumerate(array.shape)]
        where[longest] = (where[longest] + shift) % array.shape[longest]
        spots.append(tuple(where))
    return array.at[spots[0]].set(smallest).at[spots[1]].set(high)


def level_of(rng, shape, shards, smallest, top_value):
    factor_of, own = 1.0, jax.random.fold_in(rng, 6)
    for axis_at, shards_of in shards:
        steps = jnp.exp(jax.random.uniform(jax.random.fold_in(own, axis_at), (shards_of,), jnp.float32, smallest / len(shards), top_value / len(shards)))
        factor_of = factor_of * jnp.repeat(steps, shape[axis_at] // shards_of).reshape([-1 if axis == axis_at else 1 for axis in range(len(shape))])
    return factor_of


def profile(number_of, total, limit, slope):
    weights = [(1 << 20) // math.isqrt(grade ** slope) + 1 for grade in range(2, number_of + 1)]
    surplus, holding = total - limit - (number_of - 1), [1] * (number_of - 1)
    while surplus > 0:
        free = [i for i in range(number_of - 1) if holding[i] < limit]
        pool, budget = sum([weights[i] for i in free]), surplus
        for i in free:
            more = min(limit - holding[i], max(1, budget * weights[i] // pool), surplus)
            holding[i] = holding[i] + more
            surplus = surplus - more
    return np.array([limit] + holding)


def uneven(key, number_of, total, bound, skew):
    if number_of == 2:
        one = jax.random.randint(key, (), max(1, total - bound), min(bound, total - 1) + 1)
        return jnp.stack([one, total - one])
    lengths = jnp.asarray(profile(number_of, total, bound, skew), jnp.int32)
    couples = (number_of - 1) // 2
    source_of, sink = lengths[1:1 + 2 * couples:2], lengths[2:2 + 2 * couples:2]
    slack = jnp.minimum(source_of - 1, bound - sink)
    passed = jax.random.randint(jax.random.fold_in(key, 1), (couples,), 0, 1 << 20) % (slack + 1)
    lengths = lengths.at[1:1 + 2 * couples:2].set(source_of - passed).at[2:2 + 2 * couples:2].set(sink + passed)
    return lengths[jax.random.permutation(jax.random.fold_in(key, 2), number_of)]


def deal_out(rng, own, number, rows, number_of, top, limit, slope):
    sequence = jax.random.permutation(rng, number_of)
    crowded, common = portions_of(number_of, rows * top, limit, slope, True), portions_of(number_of, rows * top, limit, slope, False)
    places = jnp.arange(number_of)

    def named(sizes, offset_by):
        used = int((sizes > 0).sum())
        fixed = max(1, used // 4)
        moved = fixed + (places - fixed + offset_by * (used - fixed)) % max(1, number_of - fixed)
        return jnp.zeros((number_of,), jnp.int32).at[sequence[jnp.where(places < fixed, places, moved)]].set(jnp.asarray(sizes, jnp.int32))

    sizes = jnp.where(number % 4 == 0, named(crowded, number // 4), named(common, number - number // 4 - 1))
    mixed = jax.random.permutation(jax.random.fold_in(own, 3), number_of)
    source_of, sink = mixed[0:number_of // 2 * 2:2], mixed[1:number_of // 2 * 2:2]
    room = jnp.minimum(sizes[source_of] - 1, limit - sizes[sink]) // 2
    room = jnp.where((source_of == sequence[0]) | (sink == sequence[0]) | (sizes[sink] == 0), 0, jnp.maximum(room, 0))
    moved = jax.random.randint(jax.random.fold_in(own, 4), (number_of // 2,), 0, 1 << 20) % (room + 1)
    sizes = sizes.at[source_of].add(-moved).at[sink].add(moved)
    items = jnp.searchsorted(jnp.cumsum(sizes), jnp.arange(rows * top), side="right").astype(jnp.int32)
    grid = items.reshape(top, rows).T
    grid = grid[jax.random.permutation(jax.random.fold_in(own, 1), rows)]
    offset_by = jax.random.randint(jax.random.fold_in(own, 2), (rows, 1), 0, top)
    return jnp.take_along_axis(grid, (jnp.arange(top)[None, :] + offset_by) % top, axis=1)


def portions_of(amount, total, limit, slope, full):
    portions = [(1 << 20) // math.isqrt(grade ** slope) + 1 for grade in range(1, amount + 1)]
    largest = limit if full else min(limit, max(-(-total // amount), total * portions[0] // sum(portions)))
    least = 1 if total - largest >= amount - 1 else 0
    holding, spare = [largest] + [least] * (amount - 1), total - largest - least * (amount - 1)
    while spare > 0:
        candidates = [i for i in range(1, amount) if holding[i] < largest] or [i for i in range(1, amount) if holding[i] < limit]
        mass, budget = sum([portions[i] for i in candidates]), spare
        for i in candidates:
            addition = min(limit - holding[i], max(1, budget * portions[i] // mass), spare)
            holding[i] = holding[i] + addition
            spare = spare - addition
    return np.array(holding)


def scatter_about(stream_key, extent, width, limit, cuts=(), kind=jnp.bfloat16):
    result = width * jax.random.normal(stream_key, extent, jnp.float32)
    if cuts:
        result = result * level_of(stream_key, extent, cuts, -0.22, 0.18)
    return jnp.clip(result, -limit, limit).astype(kind)


def setup_inputs(seed: int = 0) -> dict:
    splits = jax.random.split(jax.random.key(seed), 14)
    queries = draw_queries(jax.random.fold_in(splits[13], 71), 0)
    latent = draw_latent(jax.random.fold_in(splits[13], 71), 0)
    frames = jnp.searchsorted(jnp.cumsum(uneven(splits[2], FRAMES, SEQ, TOK_DEV, 1)), jnp.arange(SEQ), side="right").astype(jnp.int32)
    w_uv = scatter_about(splits[3], (HEADS, DL, DV), (DL // 4) ** -0.5, 0.5, ((0, 8),))
    w_out = scatter_about(splits[4], (HEADS * DV, D), (HEADS * DV // 16) ** -0.5, 0.25, ((0, 8), (1, 4)))
    residual = draw_residual(jax.random.fold_in(splits[13], 71), 0)
    norm_gain = jnp.clip(jnp.exp(jax.random.uniform(splits[6], (D,), jnp.float32, math.log(0.5), math.log(2.0))), 0.5, 2.0)
    expert_ids_keys = jax.random.split(jax.random.fold_in(splits[7], 1), SEQ // TOK_DEV)
    expert_ids_turns = jax.random.permutation(jax.random.fold_in(splits[7], 3), SEQ // TOK_DEV)
    expert_ids = jax.vmap(lambda own, number: deal_out(jax.random.fold_in(splits[7], 2), own, number, TOK_DEV, EXPERTS, TOPK, CAP, 2))(expert_ids_keys, expert_ids_turns).reshape((SEQ, TOPK))
    mix_codes = plant(jax.random.randint(splits[8], (SEQ, TOPK), 1, 257), jax.random.fold_in(splits[8], 1), 1, 256).astype(jnp.int32)
    w_gate = scatter_about(splits[9], (EXPERTS, D, FE), D ** -0.5, 0.0625, ((0, 4), (2, 8)))
    w_up = scatter_about(splits[10], (EXPERTS, D, FE), D ** -0.5, 0.0625, ((0, 4), (2, 8)))
    w_down = scatter_about(splits[11], (EXPERTS, FE, D), (FE // 4) ** -0.5, 0.375, ((0, 4), (1, 8)))
    grad_out = scatter_about(splits[12], (SEQ, D), 1.0, 6.0, ((0, 4), (1, 8)))
    return dict(queries=queries, latent=latent, frames=frames, w_uv=w_uv, w_out=w_out, residual=residual, norm_gain=norm_gain, expert_ids=expert_ids, mix_codes=mix_codes, w_gate=w_gate, w_up=w_up, w_down=w_down, grad_out=grad_out)


def settle(value):
    return lax.optimization_barrier(value.astype(jnp.bfloat16)).astype(jnp.float32)

def attend_head(query_head, latent, visible, uv_head):
    scores = jnp.dot(query_head, latent.T, preferred_element_type=jnp.float32) * DL ** (-0.5)
    scores = jnp.where(visible, scores, -1e+30)
    row_top = lax.optimization_barrier(jnp.max(scores, axis=-1, keepdims=True))
    exp_scores = jnp.exp(scores - row_top)
    attn_weights = (exp_scores / lax.optimization_barrier(jnp.sum(exp_scores, axis=-1, keepdims=True))).astype(jnp.bfloat16)
    latent_mix = jnp.dot(attn_weights, latent, preferred_element_type=jnp.float32).astype(jnp.bfloat16)
    return jnp.dot(latent_mix, uv_head, preferred_element_type=jnp.float32).astype(jnp.bfloat16)

def reference(queries, latent, frames, w_uv, w_out, residual, norm_gain, expert_ids, mix_codes, w_gate, w_up, w_down, grad_out):
    visible = frames[None, :] <= frames[:, None]
    per_head = jnp.transpose(queries.reshape(SEQ, HEADS, DL), (1, 0, 2))
    head_out = lax.map(lambda head_pair: attend_head(head_pair[0], latent, visible, head_pair[1]), (per_head, w_uv))
    head_out = jnp.transpose(head_out, (1, 0, 2)).reshape(SEQ, HEADS * DV)
    group_rows = HEADS * DV // GROUPS
    attn_sum = jnp.zeros((SEQ, D), jnp.float32)
    for group_index in range(GROUPS):
        lower = group_index * group_rows
        upper = lower + group_rows
        attn_sum = attn_sum + settle(jnp.dot(head_out[:, lower:upper], w_out[lower:upper], preferred_element_type=jnp.float32))
    pre_norm = (residual.astype(jnp.float32) + attn_sum).astype(jnp.bfloat16)
    pre_full = pre_norm.astype(jnp.float32)
    inv_scale = lax.rsqrt(lax.optimization_barrier(jnp.mean(pre_full * pre_full, axis=-1, keepdims=True)) + 1e-06)
    unit_rows = pre_full * inv_scale
    normed = (unit_rows * norm_gain).astype(jnp.bfloat16)
    code_values = mix_codes.astype(jnp.float32)
    mix_weight = code_values / lax.optimization_barrier(jnp.sum(code_values, axis=1, keepdims=True))
    mix_flat = mix_weight.reshape(-1)
    chosen = expert_ids.reshape(-1)
    pair_index = jnp.arange(SEQ * TOPK, dtype=jnp.int32)
    most_rows = N_CTX * CAP
    hidden_rows = FE // GROUPS

    def expert_pass(expert_item):
        expert, gate_weight, up_weight, down_weight = expert_item
        order_key = jnp.where(chosen == expert, pair_index, pair_index + SEQ * TOPK)
        row_order = jnp.argsort(order_key)[:most_rows].astype(jnp.int32)
        filled = chosen[row_order] == expert
        token_index = row_order // TOPK
        weight = jnp.where(filled, mix_flat[row_order], 0.0)
        expert_rows = jnp.where(filled[:, None], normed[token_index], jnp.zeros((), jnp.bfloat16))
        gate_in = jnp.dot(expert_rows, gate_weight, preferred_element_type=jnp.float32)
        up_in = jnp.dot(expert_rows, up_weight, preferred_element_type=jnp.float32)
        hidden = (jax.nn.silu(gate_in) * up_in).astype(jnp.bfloat16)
        down_total = jnp.zeros((most_rows, D), jnp.float32)
        for group_index in range(GROUPS):
            lower = group_index * hidden_rows
            upper = lower + hidden_rows
            down_total = down_total + settle(jnp.dot(hidden[:, lower:upper], down_weight[lower:upper], preferred_element_type=jnp.float32))
        expert_out = down_total.astype(jnp.bfloat16)
        out_grad = (weight[:, None] * grad_out[token_index].astype(jnp.float32)).astype(jnp.bfloat16)
        hidden_grad = jnp.dot(out_grad, down_weight.T, preferred_element_type=jnp.float32)
        gate_sig = jax.nn.sigmoid(gate_in)
        gate_grad = (hidden_grad * up_in * gate_sig * (1.0 + gate_in * (1.0 - gate_sig))).astype(jnp.bfloat16)
        up_grad = (hidden_grad * jax.nn.silu(gate_in)).astype(jnp.bfloat16)
        grad_down = jnp.dot(hidden.T, out_grad, preferred_element_type=jnp.float32).astype(jnp.bfloat16)
        grad_gate = jnp.dot(expert_rows.T, gate_grad, preferred_element_type=jnp.float32).astype(jnp.bfloat16)
        grad_up = jnp.dot(expert_rows.T, up_grad, preferred_element_type=jnp.float32).astype(jnp.bfloat16)
        grad_total = jnp.zeros((most_rows, D), jnp.float32)
        for group_index in range(GROUPS):
            lower = group_index * hidden_rows
            upper = lower + hidden_rows
            gate_part = jnp.dot(gate_grad[:, lower:upper], gate_weight[:, lower:upper].T, preferred_element_type=jnp.float32)
            up_part = jnp.dot(up_grad[:, lower:upper], up_weight[:, lower:upper].T, preferred_element_type=jnp.float32)
            grad_total = grad_total + settle(gate_part + up_part)
        row_grad = grad_total.astype(jnp.bfloat16)
        return (token_index, weight, expert_out, row_grad, grad_gate, grad_up, grad_down)
    experts_range = jnp.arange(EXPERTS, dtype=jnp.int32)
    token_all, weight_all, out_all, grad_all, grad_gate, grad_up, grad_down = lax.map(expert_pass, (experts_range, w_gate, w_up, w_down))
    flat_tokens = token_all.reshape(-1)
    routed = jnp.zeros((SEQ, D), jnp.float32).at[flat_tokens].add(weight_all.reshape(-1)[:, None] * out_all.reshape(-1, D).astype(jnp.float32))
    layer_out = (pre_full + routed).astype(jnp.bfloat16)
    normed_grad = jnp.zeros((SEQ, D), jnp.float32).at[flat_tokens].add(grad_all.reshape(-1, D).astype(jnp.float32)).astype(jnp.bfloat16)
    scaled_grad = normed_grad.astype(jnp.float32) * norm_gain
    center = lax.optimization_barrier(jnp.mean(scaled_grad * unit_rows, axis=-1, keepdims=True))
    grad_pre_norm = (grad_out.astype(jnp.float32) + inv_scale * (scaled_grad - unit_rows * center)).astype(jnp.bfloat16)
    return (layer_out, grad_pre_norm, grad_gate, grad_up, grad_down)
```

```python
import jax
import jax.numpy as jnp
from jax import lax
from jax.sharding import PartitionSpec as P

GROUP = ("role", "exp")
F32 = jnp.float32
BF16 = jnp.bfloat16


def context_swap(blocks):
    return lax.all_to_all(blocks, "ctx", split_axis=0, concat_axis=0, tiled=True)


def group_sum(terms):
    return lax.psum_scatter(terms, GROUP, scatter_dimension=1, tiled=True)


def group_gather(columns):
    return lax.all_gather(columns, GROUP, axis=1, tiled=True)


def mm(a, b, dims):
    return lax.dot_general(a, b, (dims, ((), ())), preferred_element_type=F32)


def per_device(
    queries,
    latent,
    frames,
    w_uv,
    w_out,
    residual,
    norm_gain,
    expert_ids,
    mix_codes,
    w_gate,
    w_up,
    w_down,
    grad_out,
):
    ctx_count = lax.axis_size("ctx")
    ctx_place = lax.axis_index("ctx")
    group_place = lax.axis_index(GROUP)
    token_count = queries.shape[0]
    head_count, latent_width, value_width = w_uv.shape
    slice_width = residual.shape[1]
    model_width = norm_gain.shape[0]
    hidden_width = w_gate.shape[2]
    top_count = expert_ids.shape[1]
    capacity = token_count * top_count // ctx_count * 5 // 4
    slot_total = ctx_count * capacity

    expert_range = jnp.arange(ctx_count, dtype=jnp.int32)
    hits = expert_ids[:, :, None] == expert_range[None, None, :]
    hit = jnp.any(hits, axis=1).astype(F32)
    rows = jnp.arange(token_count, dtype=jnp.int32)
    before = (rows[None, :] < rows[:, None]).astype(BF16)
    rank = mm(hit.astype(BF16).T, before, ((1,), (1,)))
    code_values = mix_codes.astype(F32)
    mix_weight = code_values / jnp.sum(code_values, axis=1, keepdims=True)
    pair_weight = jnp.sum(jnp.where(hits, mix_weight[:, :, None], 0.0), axis=1)
    slot_range = jnp.arange(capacity, dtype=jnp.int32).astype(F32)
    place = (rank[:, None, :] == slot_range[None, :, None]) & (hit.T[:, None, :] > 0)
    slot_weight = jnp.sum(jnp.where(place, pair_weight.T[:, None, :], 0.0), axis=2).reshape(
        slot_total, 1
    )
    place = place.astype(BF16).reshape(slot_total, token_count)

    def to_experts(slot_rows):
        outgoing = slot_rows.astype(BF16).reshape(ctx_count, capacity, slice_width)
        return group_gather(context_swap(outgoing).reshape(slot_total, slice_width))

    def from_experts(partial_rows):
        summed = group_sum(partial_rows.astype(BF16))
        return context_swap(summed.reshape(ctx_count, capacity, slice_width)).reshape(
            slot_total, slice_width
        )

    out_grad = to_experts(mm(place, grad_out, ((1,), (0,))) * slot_weight)
    down_weight = w_down[0]
    hidden_grad = mm(out_grad, down_weight, ((1,), (1,)))
    gate_up = (
        jnp.concatenate([w_gate[0], w_up[0]], axis=1).astype(F32) * norm_gain[:, None]
    ).astype(BF16)

    key_rows = lax.all_gather(latent, "ctx", axis=0, tiled=True)
    own_frames = lax.dynamic_slice_in_dim(frames, ctx_place * token_count, token_count)
    visible = frames[None, :] <= own_frames[:, None]
    query_heads = queries.reshape(token_count, head_count, latent_width)
    scores = jnp.einsum(
        "thd,sd->hts", query_heads, key_rows, preferred_element_type=F32
    ) * latent_width ** (-0.5)
    scores = jnp.where(visible[None, :, :], scores, -1e30)
    row_top = jnp.max(scores, axis=-1, keepdims=True)
    exp_scores = jnp.exp(scores - row_top)
    attn_weights = (exp_scores / jnp.sum(exp_scores, axis=-1, keepdims=True)).astype(BF16)
    latent_mix = jnp.einsum(
        "hts,sd->thd", attn_weights, key_rows, preferred_element_type=F32
    ).astype(BF16)
    head_out = jnp.einsum(
        "thd,hdv->thv", latent_mix, w_uv, preferred_element_type=F32
    ).astype(BF16)
    head_out = head_out.reshape(token_count, head_count * value_width)
    column_part = jnp.dot(
        lax.all_gather(head_out, "ctx", axis=0, tiled=True), w_out, preferred_element_type=F32
    ).astype(BF16)
    column_width = column_part.shape[1]
    row_blocks = context_swap(column_part.reshape(ctx_count, token_count, column_width))
    row_part = jnp.transpose(row_blocks, (1, 0, 2)).reshape(token_count, ctx_count * column_width)
    attn_sum = group_sum(row_part).astype(F32)
    pre_norm = (residual.astype(F32) + attn_sum).astype(BF16)
    pre_wide = pre_norm.astype(F32)
    inv_scale = lax.rsqrt(
        lax.psum(jnp.sum(pre_wide * pre_wide, axis=1, keepdims=True), GROUP) / model_width + 1e-06
    )

    pre_rows = to_experts(mm(place, pre_norm, ((1,), (0,))))
    rows_wide = pre_rows.astype(F32)
    row_inv = lax.rsqrt(jnp.mean(rows_wide * rows_wide, axis=1, keepdims=True) + 1e-06)
    both_in = mm(pre_rows, gate_up, ((1,), (0,))) * row_inv
    gate_in = both_in[:, :hidden_width]
    up_in = both_in[:, hidden_width:]
    gate_sig = jax.nn.sigmoid(gate_in)
    gate_act = gate_in * gate_sig
    hidden = (gate_act * up_in).astype(BF16)
    gate_grad = hidden_grad * up_in * gate_sig * (1.0 + gate_in * (1.0 - gate_sig))
    up_grad = hidden_grad * gate_act
    both_grad = jnp.concatenate([gate_grad, up_grad], axis=1)
    row_back = from_experts(mm(both_grad.astype(BF16), gate_up, ((1,), (1,))))
    down_back = from_experts(mm(hidden, down_weight, ((1,), (0,))))
    grad_both = mm(pre_rows, (both_grad * row_inv).astype(BF16), ((0,), (0,))) * norm_gain[:, None]
    grad_gate = grad_both[:, :hidden_width].astype(BF16)[None]
    grad_up = grad_both[:, hidden_width:].astype(BF16)[None]
    grad_down = mm(hidden, out_grad, ((0,), (0,))).astype(BF16)[None]

    scaled_grad = mm(place, row_back, ((0,), (0,)))
    center = (
        lax.psum(jnp.sum(scaled_grad * pre_wide, axis=1, keepdims=True), GROUP)
        * inv_scale
        / model_width
    )
    grad_pre_norm = (
        grad_out.astype(F32) + inv_scale * (scaled_grad - pre_wide * inv_scale * center)
    ).astype(BF16)
    routed = mm(place, (down_back.astype(F32) * slot_weight).astype(BF16), ((0,), (0,)))
    layer_out = (pre_wide + routed).astype(BF16)
    return (layer_out, grad_pre_norm, grad_gate, grad_up, grad_down)


def solution(mesh):
    placed = (
        P("ctx", GROUP),
        P("ctx", None),
        P(),
        P(GROUP, None, None),
        P(GROUP, "ctx"),
        P("ctx", GROUP),
        P(),
        P("ctx", None),
        P("ctx", None),
        P("ctx", None, GROUP),
        P("ctx", None, GROUP),
        P("ctx", GROUP, None),
        P("ctx", GROUP),
    )
    return jax.shard_map(
        per_device,
        mesh=mesh,
        in_specs=placed,
        out_specs=(
            P("ctx", GROUP),
            P("ctx", GROUP),
            P("ctx", None, GROUP),
            P("ctx", None, GROUP),
            P("ctx", GROUP, None),
        ),
        check_vma=False,
    )
```

```python
import jax
import jax.numpy as jnp
from jax import lax
from jax.experimental import pallas as pl
from jax.experimental.pallas import tpu as pltpu
from jax.sharding import PartitionSpec as P

GROUP = ("role", "exp")
F32 = jnp.float32
BF16 = jnp.bfloat16


def context_swap(blocks):
    return lax.all_to_all(blocks, "ctx", split_axis=0, concat_axis=0, tiled=True)


def group_sum(terms):
    return lax.psum_scatter(terms, GROUP, scatter_dimension=1, tiled=True)


def group_gather(columns):
    return lax.all_gather(columns, GROUP, axis=1, tiled=True)


def mm(a, b, dims):
    return lax.dot_general(a, b, (dims, ((), ())), preferred_element_type=F32)


def push(src, dst, send_sem, recv_sem, device):
    return pltpu.make_async_remote_copy(
        src_ref=src,
        dst_ref=dst,
        send_sem=send_sem,
        recv_sem=recv_sem,
        device_id=device,
        device_id_type=pl.DeviceIdType.MESH,
    )


def places(n_ctx, n_role, n_exp):
    c, r, z = lax.axis_index("ctx"), lax.axis_index("role"), lax.axis_index("exp")
    ctx_peers = [(lax.rem(c + k, n_ctx), r, z) for k in range(n_ctx)]
    exp_peers = [(c, r, lax.rem(z + k, n_exp)) for k in range(n_exp)]
    return c, r, z, ctx_peers, exp_peers, (c, 1 - r, z)


def greet(peers):
    barrier = pltpu.get_barrier_semaphore()
    for peer in peers:
        pl.semaphore_signal(
            barrier, inc=1, device_id=peer, device_id_type=pl.DeviceIdType.MESH
        )
    pl.semaphore_wait(barrier, len(peers))


def span(start, size):
    return pl.ds(pl.multiple_of(start * size, size), size)


def call_kernel(body, outs, scratch, number, args):
    vmem = pl.BlockSpec(memory_space=pltpu.VMEM)
    return pl.pallas_call(
        body,
        out_shape=outs,
        in_specs=[vmem] * len(args),
        out_specs=jax.tree.map(lambda _: vmem, outs),
        scratch_shapes=scratch,
        compiler_params=pltpu.CompilerParams(
            collective_id=number, has_side_effects=True, vmem_limit_bytes=58 << 20
        ),
    )(*args)


def project_out(head_out, w_out, sizes):
    n_ctx, n_role, n_exp = sizes
    tokens, depth = head_out.shape
    width = w_out.shape[1]
    half = n_ctx * tokens // n_role
    chunk = half // n_exp

    def body(head_ref, w_ref, out_ref, heads, mine, theirs, parts, got, sems, core_sems, exp_sems):
        c, r, z, ctx_peers, exp_peers, partner = places(*sizes)
        greet(ctx_peers[1:] + exp_peers[1:] + [partner])
        copies = [
            push(head_ref, heads.at[c], sems.at[0, k], sems.at[1, k], ctx_peers[k])
            for k in range(1, n_ctx)
        ]
        for copy in copies:
            copy.start()
        heads[c] = head_ref[...]
        for copy in copies:
            copy.wait()
        per_role = n_ctx // n_role
        for j in range(per_role):
            mine[pl.ds(j * tokens, tokens), :] = mm(
                heads[(1 - r) * per_role + j], w_ref[...], ((1,), (0,))
            ).astype(BF16)
        swap = push(mine, theirs, core_sems.at[0], core_sems.at[1], partner)
        swap.start()
        for j in range(per_role):
            parts[pl.ds(j * tokens, tokens), :] = mm(
                heads[r * per_role + j], w_ref[...], ((1,), (0,))
            ).astype(BF16)
        swap.wait()
        parts[...] = (parts[...].astype(F32) + theirs[...].astype(F32)).astype(BF16)
        copies = []
        for k in range(1, n_exp):
            target = lax.rem(z + k, n_exp)
            copy = push(
                parts.at[span(target, chunk), :],
                got.at[k],
                exp_sems.at[0, k],
                exp_sems.at[1, k],
                exp_peers[k],
            )
            copy.start()
            copies.append(copy)
        for copy in copies:
            copy.wait()
        total = parts[span(z, chunk), :].astype(F32)
        for k in range(1, n_exp):
            total = total + got[k].astype(F32)
        out_ref[...] = total.astype(BF16)

    return call_kernel(
        body,
        jax.ShapeDtypeStruct((chunk, width), BF16),
        [
            pltpu.VMEM((n_ctx, tokens, depth), BF16),
            pltpu.VMEM((half, width), BF16),
            pltpu.VMEM((half, width), BF16),
            pltpu.VMEM((half, width), BF16),
            pltpu.VMEM((n_exp, chunk, width), BF16),
            pltpu.SemaphoreType.DMA((2, n_ctx)),
            pltpu.SemaphoreType.DMA((2,)),
            pltpu.SemaphoreType.DMA((2, n_exp)),
        ],
        1,
        (head_out, w_out),
    )


def dispatch(place, block, sizes):
    n_ctx, n_role, n_exp = sizes
    tokens, width = block.shape
    slots = place.shape[0]
    cap = slots // n_ctx
    half = width * n_exp

    def body(place_ref, block_ref, out_ref, cols, sent, z_sems, c_sems, p_sems):
        c, r, z, ctx_peers, exp_peers, partner = places(*sizes)
        greet(ctx_peers[1:] + exp_peers[1:] + [partner])
        gathers = [None] + [
            push(block_ref, cols.at[z], z_sems.at[0, k], z_sems.at[1, k], exp_peers[k])
            for k in range(1, n_exp)
        ]
        for copy in gathers[1:]:
            copy.start()
        cols[z] = block_ref[...]
        swaps = []
        for s in range(n_exp):
            piece = lax.rem(z + s, n_exp)
            if s:
                gathers[n_exp - s].wait_recv()
            where = span(r * n_exp + piece, width)
            sent[s] = mm(place_ref[...], cols[piece], ((1,), (0,))).astype(BF16)
            for k in range(1, n_ctx):
                target = lax.rem(c + k, n_ctx)
                copy = push(
                    sent.at[s, span(target, cap), :],
                    out_ref.at[span(c, cap), where],
                    c_sems.at[0, s, k],
                    c_sems.at[1, s, k],
                    ctx_peers[k],
                )
                copy.start()
                swaps.append((s, k, where, copy))
            out_ref[span(c, cap), where] = sent[s, span(c, cap), :]
        moves = []
        for s in range(n_exp):
            where = span(r * n_exp + lax.rem(z + s, n_exp), width)
            for k in range(n_ctx):
                if k:
                    swaps[s * (n_ctx - 1) + k - 1][3].wait_recv()
                region = out_ref.at[span(lax.rem(c + n_ctx - k, n_ctx), cap), where]
                move = push(region, region, p_sems.at[0, s, k], p_sems.at[1, s, k], partner)
                move.start()
                moves.append(move)
        for copy in gathers[1:]:
            copy.wait_send()
        for item in swaps:
            item[3].wait_send()
        for move in moves:
            move.wait()

    return call_kernel(
        body,
        jax.ShapeDtypeStruct((slots, half * n_role), BF16),
        [
            pltpu.VMEM((n_exp, tokens, width), BF16),
            pltpu.VMEM((n_exp, slots, width), BF16),
            pltpu.SemaphoreType.DMA((2, n_exp)),
            pltpu.SemaphoreType.DMA((2, n_exp, n_ctx)),
            pltpu.SemaphoreType.DMA((2, n_exp, n_ctx)),
        ],
        2,
        (place, block),
    )


def combine(place, slot_weight, row_part, down_part, sizes):
    n_ctx, n_role, n_exp = sizes
    slots, tokens = place.shape
    cap = slots // n_ctx
    width = row_part.shape[1] // (n_role * n_exp)

    def body(
        place_ref, weight_ref, row_ref, down_ref, row_out, down_out, theirs, sent, got, back, last,
        p_sems, c_sems, z_sems,
    ):
        c, r, z, ctx_peers, exp_peers, partner = places(*sizes)
        greet(ctx_peers[1:] + exp_peers[1:] + [partner])
        order = [(i, s) for i in range(2) for s in list(range(1, n_exp)) + [0]]
        sources = (row_ref, down_ref)
        firsts, swaps, finals = {}, {}, []
        for i, s in order:
            piece = lax.rem(z + s, n_exp)
            firsts[i, s] = push(
                sources[i].at[:, span((1 - r) * n_exp + piece, width)],
                theirs.at[i, s],
                p_sems.at[0, i, s],
                p_sems.at[1, i, s],
                partner,
            )
            firsts[i, s].start()
        for i, s in order:
            piece = lax.rem(z + s, n_exp)
            firsts[i, s].wait_recv()
            own = sources[i][:, span(r * n_exp + piece, width)].astype(F32)
            sent[i, s] = (own + theirs[i, s].astype(F32)).astype(BF16)
            for k in range(1, n_ctx):
                copy = push(
                    sent.at[i, s, span(lax.rem(c + k, n_ctx), cap), :],
                    got.at[i, s, span(c, cap), :],
                    c_sems.at[0, i, s, k],
                    c_sems.at[1, i, s, k],
                    ctx_peers[k],
                )
                copy.start()
                swaps[i, s, k] = copy
            got[i, s, span(c, cap), :] = sent[i, s, span(c, cap), :]
        for i, s in order:
            for k in range(1, n_ctx):
                swaps[i, s, k].wait_recv()
            rows = got[i, s]
            if i == 1:
                rows = (rows.astype(F32) * weight_ref[...]).astype(BF16)
            merged = mm(place_ref[...], rows, ((0,), (0,)))
            if s == 0:
                (row_out, down_out)[i][...] = merged
            else:
                back[i, s] = merged.astype(BF16)
                copy = push(
                    back.at[i, s],
                    last.at[i, s],
                    z_sems.at[0, i, s],
                    z_sems.at[1, i, s],
                    exp_peers[s],
                )
                copy.start()
                finals.append((i, s, copy))
        for i, s, copy in finals:
            copy.wait_recv()
            target = (row_out, down_out)[i]
            target[...] = target[...] + last[i, s].astype(F32)
        for copy in list(firsts.values()) + list(swaps.values()) + [f[2] for f in finals]:
            copy.wait_send()

    out = jax.ShapeDtypeStruct((tokens, width), F32)
    return call_kernel(
        body,
        (out, out),
        [
            pltpu.VMEM((2, n_exp, slots, width), BF16),
            pltpu.VMEM((2, n_exp, slots, width), BF16),
            pltpu.VMEM((2, n_exp, slots, width), BF16),
            pltpu.VMEM((2, n_exp, tokens, width), BF16),
            pltpu.VMEM((2, n_exp, tokens, width), BF16),
            pltpu.SemaphoreType.DMA((2, 2, n_exp)),
            pltpu.SemaphoreType.DMA((2, 2, n_exp, n_ctx)),
            pltpu.SemaphoreType.DMA((2, 2, n_exp)),
        ],
        3,
        (place, slot_weight, row_part, down_part),
    )


def reorder(chunk, sizes, slice_width):
    n_ctx, n_role, n_exp = sizes
    groups = n_role * n_exp
    g = lax.axis_index(GROUP)
    pieces = []
    for k in range(2):
        perm = []
        for src_c in range(n_ctx):
            for src_g in range(groups):
                target = (src_g // 2) * groups + 2 * src_c + ((src_g % 2) ^ k)
                perm.append((src_c * groups + src_g, target))
        column = ((g % 2) ^ k) * slice_width
        part = lax.dynamic_slice_in_dim(chunk, column, slice_width, 1)
        pieces.append(lax.ppermute(part, ("ctx",) + GROUP, perm))
    even = g % 2 == 0
    return jnp.concatenate(
        [jnp.where(even, pieces[0], pieces[1]), jnp.where(even, pieces[1], pieces[0])], axis=0
    )


def per_device(
    queries,
    latent,
    frames,
    w_uv,
    w_out,
    residual,
    norm_gain,
    expert_ids,
    mix_codes,
    w_gate,
    w_up,
    w_down,
    grad_out,
):
    ctx_count = lax.axis_size("ctx")
    ctx_place = lax.axis_index("ctx")
    group_place = lax.axis_index(GROUP)
    token_count = queries.shape[0]
    head_count, latent_width, value_width = w_uv.shape
    slice_width = residual.shape[1]
    model_width = norm_gain.shape[0]
    hidden_width = w_gate.shape[2]
    top_count = expert_ids.shape[1]
    capacity = token_count * top_count // ctx_count * 5 // 4
    slot_total = ctx_count * capacity
    sizes = (ctx_count, lax.axis_size("role"), lax.axis_size("exp"))
    paired = capacity % 16 == 0 and 2 * ctx_count == sizes[1] * sizes[2] and sizes[1] == 2

    expert_range = jnp.arange(ctx_count, dtype=jnp.int32)
    hits = expert_ids[:, :, None] == expert_range[None, None, :]
    hit = jnp.any(hits, axis=1).astype(F32)
    rows = jnp.arange(token_count, dtype=jnp.int32)
    before = (rows[None, :] < rows[:, None]).astype(BF16)
    rank = mm(hit.astype(BF16).T, before, ((1,), (1,)))
    code_values = mix_codes.astype(F32)
    mix_weight = code_values / jnp.sum(code_values, axis=1, keepdims=True)
    pair_weight = jnp.sum(jnp.where(hits, mix_weight[:, :, None], 0.0), axis=1)
    slot_range = jnp.arange(capacity, dtype=jnp.int32).astype(F32)
    place = (rank[:, None, :] == slot_range[None, :, None]) & (hit.T[:, None, :] > 0)
    slot_weight = jnp.sum(jnp.where(place, pair_weight.T[:, None, :], 0.0), axis=2).reshape(
        slot_total, 1
    )
    place = place.astype(BF16).reshape(slot_total, token_count)

    def to_experts(slot_rows):
        outgoing = slot_rows.astype(BF16).reshape(ctx_count, capacity, slice_width)
        return group_gather(context_swap(outgoing).reshape(slot_total, slice_width))

    def from_experts(partial_rows):
        summed = group_sum(partial_rows.astype(BF16))
        return context_swap(summed.reshape(ctx_count, capacity, slice_width)).reshape(
            slot_total, slice_width
        )

    out_grad = to_experts(mm(place, grad_out, ((1,), (0,))) * slot_weight)
    down_weight = w_down[0]
    hidden_grad = mm(out_grad, down_weight, ((1,), (1,)))
    gate_up = (
        jnp.concatenate([w_gate[0], w_up[0]], axis=1).astype(F32) * norm_gain[:, None]
    ).astype(BF16)

    key_rows = lax.all_gather(latent, "ctx", axis=0, tiled=True)
    own_frames = lax.dynamic_slice_in_dim(frames, ctx_place * token_count, token_count)
    visible = frames[None, :] <= own_frames[:, None]
    query_heads = queries.reshape(token_count, head_count, latent_width)
    scores = jnp.einsum(
        "thd,sd->hts", query_heads, key_rows, preferred_element_type=F32
    ) * latent_width ** (-0.5)
    scores = jnp.where(visible[None, :, :], scores, -1e30)
    row_top = jnp.max(scores, axis=-1, keepdims=True)
    exp_scores = jnp.exp(scores - row_top)
    attn_weights = (exp_scores / jnp.sum(exp_scores, axis=-1, keepdims=True)).astype(BF16)
    latent_mix = jnp.einsum(
        "hts,sd->thd", attn_weights, key_rows, preferred_element_type=F32
    ).astype(BF16)
    head_out = jnp.einsum(
        "thd,hdv->thv", latent_mix, w_uv, preferred_element_type=F32
    ).astype(BF16)
    head_out = head_out.reshape(token_count, head_count * value_width)
    if paired:
        attn_sum = reorder(project_out(head_out, w_out, sizes), sizes, slice_width).astype(F32)
    else:
        column_part = jnp.dot(
            lax.all_gather(head_out, "ctx", axis=0, tiled=True), w_out, preferred_element_type=F32
        ).astype(BF16)
        column_width = column_part.shape[1]
        row_blocks = context_swap(column_part.reshape(ctx_count, token_count, column_width))
        row_part = jnp.transpose(row_blocks, (1, 0, 2)).reshape(token_count, ctx_count * column_width)
        attn_sum = group_sum(row_part).astype(F32)
    pre_norm = (residual.astype(F32) + attn_sum).astype(BF16)
    pre_wide = pre_norm.astype(F32)
    inv_scale = lax.rsqrt(
        lax.psum(jnp.sum(pre_wide * pre_wide, axis=1, keepdims=True), GROUP) / model_width + 1e-06
    )

    if paired:
        pre_rows = dispatch(place, pre_norm, sizes)
    else:
        pre_rows = to_experts(mm(place, pre_norm, ((1,), (0,))))
    rows_wide = pre_rows.astype(F32)
    row_inv = lax.rsqrt(jnp.mean(rows_wide * rows_wide, axis=1, keepdims=True) + 1e-06)
    both_in = mm(pre_rows, gate_up, ((1,), (0,))) * row_inv
    gate_in = both_in[:, :hidden_width]
    up_in = both_in[:, hidden_width:]
    gate_sig = jax.nn.sigmoid(gate_in)
    gate_act = gate_in * gate_sig
    hidden = (gate_act * up_in).astype(BF16)
    gate_grad = hidden_grad * up_in * gate_sig * (1.0 + gate_in * (1.0 - gate_sig))
    up_grad = hidden_grad * gate_act
    both_grad = jnp.concatenate([gate_grad, up_grad], axis=1)
    row_part = mm(both_grad.astype(BF16), gate_up, ((1,), (1,))).astype(BF16)
    down_part = mm(hidden, down_weight, ((1,), (0,))).astype(BF16)
    if paired:
        scaled_grad, routed = combine(place, slot_weight, row_part, down_part, sizes)
    else:
        scaled_grad = mm(place, from_experts(row_part), ((0,), (0,)))
        down_back = from_experts(down_part).astype(F32) * slot_weight
        routed = mm(place, down_back.astype(BF16), ((0,), (0,)))
    grad_both = mm(pre_rows, (both_grad * row_inv).astype(BF16), ((0,), (0,))) * norm_gain[:, None]
    grad_gate = grad_both[:, :hidden_width].astype(BF16)[None]
    grad_up = grad_both[:, hidden_width:].astype(BF16)[None]
    grad_down = mm(hidden, out_grad, ((0,), (0,))).astype(BF16)[None]

    center = (
        lax.psum(jnp.sum(scaled_grad * pre_wide, axis=1, keepdims=True), GROUP)
        * inv_scale
        / model_width
    )
    grad_pre_norm = (
        grad_out.astype(F32) + inv_scale * (scaled_grad - pre_wide * inv_scale * center)
    ).astype(BF16)
    layer_out = (pre_wide + routed).astype(BF16)
    return (layer_out, grad_pre_norm, grad_gate, grad_up, grad_down)


def solution(mesh):
    placed = (
        P("ctx", GROUP),
        P("ctx", None),
        P(),
        P(GROUP, None, None),
        P(GROUP, "ctx"),
        P("ctx", GROUP),
        P(),
        P("ctx", None),
        P("ctx", None),
        P("ctx", None, GROUP),
        P("ctx", None, GROUP),
        P("ctx", GROUP, None),
        P("ctx", GROUP),
    )
    return jax.shard_map(
        per_device,
        mesh=mesh,
        in_specs=placed,
        out_specs=(
            P("ctx", GROUP),
            P("ctx", GROUP),
            P("ctx", None, GROUP),
            P("ctx", None, GROUP),
            P("ctx", GROUP, None),
        ),
        check_vma=False,
    )
```

```python
import jax
import jax.numpy as jnp
from jax import lax
from jax.experimental import pallas as pl
from jax.experimental.pallas import tpu as pltpu
from jax.sharding import PartitionSpec as P

GROUP = ("role", "exp")
F32 = jnp.float32
BF16 = jnp.bfloat16


def context_swap(blocks):
    return lax.all_to_all(blocks, "ctx", split_axis=0, concat_axis=0, tiled=True)


def group_sum(terms):
    return lax.psum_scatter(terms, GROUP, scatter_dimension=1, tiled=True)


def group_gather(columns):
    return lax.all_gather(columns, GROUP, axis=1, tiled=True)


def mm(a, b, dims):
    return lax.dot_general(a, b, (dims, ((), ())), preferred_element_type=F32)


def push(src, dst, send_sem, recv_sem, device):
    return pltpu.make_async_remote_copy(
        src_ref=src,
        dst_ref=dst,
        send_sem=send_sem,
        recv_sem=recv_sem,
        device_id=device,
        device_id_type=pl.DeviceIdType.MESH,
    )


def places(n_ctx, n_role, n_exp):
    c, r, z = lax.axis_index("ctx"), lax.axis_index("role"), lax.axis_index("exp")
    ctx_peers = [(lax.rem(c + k, n_ctx), r, z) for k in range(n_ctx)]
    exp_peers = [(c, r, lax.rem(z + k, n_exp)) for k in range(n_exp)]
    return c, r, z, ctx_peers, exp_peers, (c, 1 - r, z)


def greet(peers):
    barrier = pltpu.get_barrier_semaphore()
    for peer in peers:
        pl.semaphore_signal(
            barrier, inc=1, device_id=peer, device_id_type=pl.DeviceIdType.MESH
        )
    pl.semaphore_wait(barrier, len(peers))


def span(start, size):
    return pl.ds(pl.multiple_of(start * size, size), size)


def call_kernel(body, outs, scratch, number, args):
    vmem = pl.BlockSpec(memory_space=pltpu.VMEM)
    return pl.pallas_call(
        body,
        out_shape=outs,
        in_specs=[vmem] * len(args),
        out_specs=jax.tree.map(lambda _: vmem, outs),
        scratch_shapes=scratch,
        compiler_params=pltpu.CompilerParams(
            collective_id=number, has_side_effects=True, vmem_limit_bytes=58 << 20
        ),
    )(*args)


def project_out(head_out, w_out, place, slot_weight, block, sizes):
    n_ctx, n_role, n_exp = sizes
    tokens, depth = head_out.shape
    width = w_out.shape[1]
    half = n_ctx * tokens // n_role
    chunk = half // n_exp
    slice_width = block.shape[1]
    slots = place.shape[0]
    cap = slots // n_ctx

    def body(
        head_ref, w_ref, place_ref, weight_ref, block_ref, out_ref, slot_ref,
        heads, mine, theirs, parts, got, done, cols, sent,
        sems, core_sems, exp_sems, shuffle_sems, g_sems, c_sems, p_sems,
    ):
        c, r, z, ctx_peers, exp_peers, partner = places(*sizes)
        g = r * n_exp + z
        away = c != g // 2
        owners = []
        for k in range(2):
            to = 2 * c + lax.rem(g + k, 2)
            owners.append((g // 2, to // n_exp, lax.rem(to, n_exp)))
        barrier = pltpu.get_barrier_semaphore()
        for peer in ctx_peers[1:] + exp_peers[1:] + [partner, owners[1]]:
            pl.semaphore_signal(
                barrier, inc=1, device_id=peer, device_id_type=pl.DeviceIdType.MESH
            )

        @pl.when(away)
        def _():
            pl.semaphore_signal(
                barrier, inc=1, device_id=owners[0], device_id_type=pl.DeviceIdType.MESH
            )

        pl.semaphore_wait(barrier, n_ctx + n_exp + jnp.where(away, 1, 0))
        copies = [
            push(head_ref, heads.at[c], sems.at[0, k], sems.at[1, k], ctx_peers[k])
            for k in range(1, n_ctx)
        ]
        for copy in copies:
            copy.start()
        heads[c] = head_ref[...]
        gathers = [None] + [
            push(block_ref, cols.at[z], g_sems.at[0, k], g_sems.at[1, k], exp_peers[k])
            for k in range(1, n_exp)
        ]
        for copy in gathers[1:]:
            copy.start()
        cols[z] = block_ref[...]
        for copy in copies:
            copy.wait()
        per_role = n_ctx // n_role
        for j in range(per_role):
            mine[pl.ds(j * tokens, tokens), :] = mm(
                heads[(1 - r) * per_role + j], w_ref[...], ((1,), (0,))
            ).astype(BF16)
        swap = push(mine, theirs, core_sems.at[0], core_sems.at[1], partner)
        swap.start()
        for j in range(per_role):
            parts[pl.ds(j * tokens, tokens), :] = mm(
                heads[r * per_role + j], w_ref[...], ((1,), (0,))
            ).astype(BF16)
        swaps = []
        for s in range(n_exp):
            piece = lax.rem(z + s, n_exp)
            if s:
                gathers[n_exp - s].wait_recv()
            where = span(r * n_exp + piece, slice_width)
            rows = mm(place_ref[...], cols[piece], ((1,), (0,))) * weight_ref[...]
            sent[s] = rows.astype(BF16)
            for k in range(1, n_ctx):
                copy = push(
                    sent.at[s, span(lax.rem(c + k, n_ctx), cap), :],
                    slot_ref.at[span(c, cap), where],
                    c_sems.at[0, s, k],
                    c_sems.at[1, s, k],
                    ctx_peers[k],
                )
                copy.start()
                swaps.append(copy)
            slot_ref[span(c, cap), where] = sent[s, span(c, cap), :]
        swap.wait()
        parts[...] = (parts[...].astype(F32) + theirs[...].astype(F32)).astype(BF16)
        copies = []
        for k in range(1, n_exp):
            target = lax.rem(z + k, n_exp)
            copy = push(
                parts.at[span(target, chunk), :],
                got.at[k],
                exp_sems.at[0, k],
                exp_sems.at[1, k],
                exp_peers[k],
            )
            copy.start()
            copies.append(copy)
        for copy in copies:
            copy.wait()
        total = parts[span(z, chunk), :].astype(F32)
        for k in range(1, n_exp):
            total = total + got[k].astype(F32)
        done[...] = total.astype(BF16)
        shuffles = []
        for k in range(2):
            shuffles.append(
                push(
                    done.at[:, span(lax.rem(g + k, 2), slice_width)],
                    out_ref.at[span(lax.rem(g, 2), chunk), :],
                    shuffle_sems.at[0, k],
                    shuffle_sems.at[1, k],
                    owners[k],
                )
            )
        shuffles[1].start()

        @pl.when(away)
        def _():
            shuffles[0].start()

        @pl.when(jnp.logical_not(away))
        def _():
            out_ref[span(lax.rem(g, 2), chunk), :] = done[:, span(lax.rem(g, 2), slice_width)]

        moves = []
        for s in range(n_exp):
            where = span(r * n_exp + lax.rem(z + s, n_exp), slice_width)
            for k in range(n_ctx):
                if k:
                    swaps[s * (n_ctx - 1) + k - 1].wait_recv()
                region = slot_ref.at[span(lax.rem(c + n_ctx - k, n_ctx), cap), where]
                move = push(region, region, p_sems.at[0, s, k], p_sems.at[1, s, k], partner)
                move.start()
                moves.append(move)
        for copy in gathers[1:] + swaps:
            copy.wait_send()
        for move in moves:
            move.wait()
        shuffles[1].wait()

        @pl.when(away)
        def _():
            shuffles[0].wait()

    return call_kernel(
        body,
        (
            jax.ShapeDtypeStruct((tokens, slice_width), BF16),
            jax.ShapeDtypeStruct((slots, slice_width * n_role * n_exp), BF16),
        ),
        [
            pltpu.VMEM((n_ctx, tokens, depth), BF16),
            pltpu.VMEM((half, width), BF16),
            pltpu.VMEM((half, width), BF16),
            pltpu.VMEM((half, width), BF16),
            pltpu.VMEM((n_exp, chunk, width), BF16),
            pltpu.VMEM((chunk, width), BF16),
            pltpu.VMEM((n_exp, tokens, slice_width), BF16),
            pltpu.VMEM((n_exp, slots, slice_width), BF16),
            pltpu.SemaphoreType.DMA((2, n_ctx)),
            pltpu.SemaphoreType.DMA((2,)),
            pltpu.SemaphoreType.DMA((2, n_exp)),
            pltpu.SemaphoreType.DMA((2, 2)),
            pltpu.SemaphoreType.DMA((2, n_exp)),
            pltpu.SemaphoreType.DMA((2, n_exp, n_ctx)),
            pltpu.SemaphoreType.DMA((2, n_exp, n_ctx)),
        ],
        1,
        (head_out, w_out, place, slot_weight, block),
    )


def dispatch(place, block, sizes):
    n_ctx, n_role, n_exp = sizes
    tokens, width = block.shape
    slots = place.shape[0]
    cap = slots // n_ctx
    half = width * n_exp

    def body(place_ref, block_ref, out_ref, cols, sent, z_sems, c_sems, p_sems):
        c, r, z, ctx_peers, exp_peers, partner = places(*sizes)
        greet(ctx_peers[1:] + exp_peers[1:] + [partner])
        gathers = [None] + [
            push(block_ref, cols.at[z], z_sems.at[0, k], z_sems.at[1, k], exp_peers[k])
            for k in range(1, n_exp)
        ]
        for copy in gathers[1:]:
            copy.start()
        cols[z] = block_ref[...]
        swaps = []
        for s in range(n_exp):
            piece = lax.rem(z + s, n_exp)
            if s:
                gathers[n_exp - s].wait_recv()
            where = span(r * n_exp + piece, width)
            sent[s] = mm(place_ref[...], cols[piece], ((1,), (0,))).astype(BF16)
            for k in range(1, n_ctx):
                target = lax.rem(c + k, n_ctx)
                copy = push(
                    sent.at[s, span(target, cap), :],
                    out_ref.at[span(c, cap), where],
                    c_sems.at[0, s, k],
                    c_sems.at[1, s, k],
                    ctx_peers[k],
                )
                copy.start()
                swaps.append((s, k, where, copy))
            out_ref[span(c, cap), where] = sent[s, span(c, cap), :]
        moves = []
        for s in range(n_exp):
            where = span(r * n_exp + lax.rem(z + s, n_exp), width)
            for k in range(n_ctx):
                if k:
                    swaps[s * (n_ctx - 1) + k - 1][3].wait_recv()
                region = out_ref.at[span(lax.rem(c + n_ctx - k, n_ctx), cap), where]
                move = push(region, region, p_sems.at[0, s, k], p_sems.at[1, s, k], partner)
                move.start()
                moves.append(move)
        for copy in gathers[1:]:
            copy.wait_send()
        for item in swaps:
            item[3].wait_send()
        for move in moves:
            move.wait()

    return call_kernel(
        body,
        jax.ShapeDtypeStruct((slots, half * n_role), BF16),
        [
            pltpu.VMEM((n_exp, tokens, width), BF16),
            pltpu.VMEM((n_exp, slots, width), BF16),
            pltpu.SemaphoreType.DMA((2, n_exp)),
            pltpu.SemaphoreType.DMA((2, n_exp, n_ctx)),
            pltpu.SemaphoreType.DMA((2, n_exp, n_ctx)),
        ],
        2,
        (place, block),
    )


def combine(place, slot_weight, both_grad, gate_up, hidden, down, pre_norm, sizes):
    n_ctx, n_role, n_exp = sizes
    slots, tokens = place.shape
    cap = slots // n_ctx
    width = pre_norm.shape[1]
    groups = n_role * n_exp

    def body(
        place_ref, weight_ref, both_ref, wide_ref, hidden_ref, down_ref, pre_ref,
        row_out, down_out, sum_out, mine, theirs, sent, got, back, last, sums,
        p_sems, c_sems, z_sems, s_sems,
    ):
        c, r, z, ctx_peers, exp_peers, partner = places(*sizes)
        group_peers = [
            (c, lax.rem(r + k // n_exp, n_role), lax.rem(z + k, n_exp)) for k in range(groups)
        ]
        greet(ctx_peers[1:] + group_peers[1:])
        order = [(i, s) for i in range(2) for s in list(range(1, n_exp)) + [0]]
        firsts, swaps, finals = {}, {}, []

        def product(i, role, piece):
            where = span(role * n_exp + piece, width)
            if i == 0:
                return mm(both_ref[...], wide_ref[where, :], ((1,), (1,)))
            return mm(hidden_ref[...], down_ref[:, where], ((1,), (0,)))

        def offer(i, s):
            mine[i, s] = product(i, 1 - r, lax.rem(z + s, n_exp)).astype(BF16)
            firsts[i, s] = push(
                mine.at[i, s], theirs.at[i, s], p_sems.at[0, i, s], p_sems.at[1, i, s], partner
            )
            firsts[i, s].start()

        offer(*order[0])
        for at, (i, s) in enumerate(order):
            if at + 1 < len(order):
                offer(*order[at + 1])
            own = product(i, r, lax.rem(z + s, n_exp))
            firsts[i, s].wait_recv()
            sent[i, s] = (own + theirs[i, s].astype(F32)).astype(BF16)
            for k in range(1, n_ctx):
                copy = push(
                    sent.at[i, s, span(lax.rem(c + k, n_ctx), cap), :],
                    got.at[i, s, span(c, cap), :],
                    c_sems.at[0, i, s, k],
                    c_sems.at[1, i, s, k],
                    ctx_peers[k],
                )
                copy.start()
                swaps[i, s, k] = copy
            got[i, s, span(c, cap), :] = sent[i, s, span(c, cap), :]
        for i, s in order:
            for k in range(1, n_ctx):
                swaps[i, s, k].wait_recv()
            rows = got[i, s]
            if i == 1:
                rows = (rows.astype(F32) * weight_ref[...]).astype(BF16)
            merged = mm(place_ref[...], rows, ((0,), (0,)))
            if s == 0:
                (row_out, down_out)[i][...] = merged
            else:
                back[i, s] = merged.astype(BF16)
                copy = push(
                    back.at[i, s],
                    last.at[i, s],
                    z_sems.at[0, i, s],
                    z_sems.at[1, i, s],
                    exp_peers[s],
                )
                copy.start()
                finals.append((i, s, copy))
        def take(item):
            for i, s, copy in finals:
                if i == item:
                    copy.wait_recv()
                    target = (row_out, down_out)[i]
                    target[...] = target[...] + last[i, s].astype(F32)

        def row_sums(values):
            return lax.dot_general(
                jnp.ones((8, width), F32),
                values,
                (((1,), (1,)), ((), ())),
                precision=lax.Precision.HIGHEST,
                preferred_element_type=F32,
            )

        take(0)
        pre = pre_ref[...].astype(F32)
        sums[0, pl.ds(0, 8), :] = row_sums(pre * pre)
        sums[0, pl.ds(8, 8), :] = row_sums(pre * row_out[...])
        shares = []
        for k in range(1, groups):
            copy = push(sums.at[0], sums.at[k], s_sems.at[0, k], s_sems.at[1, k], group_peers[k])
            copy.start()
            shares.append(copy)
        take(1)
        total = sums[0]
        for k in range(1, groups):
            shares[k - 1].wait_recv()
            total = total + sums[k]
        sum_out[...] = total
        for copy in list(firsts.values()) + list(swaps.values()) + [f[2] for f in finals]:
            copy.wait_send()
        for copy in shares:
            copy.wait_send()

    out = jax.ShapeDtypeStruct((tokens, width), F32)
    return call_kernel(
        body,
        (out, out, jax.ShapeDtypeStruct((16, tokens), F32)),
        [
            pltpu.VMEM((2, n_exp, slots, width), BF16),
            pltpu.VMEM((2, n_exp, slots, width), BF16),
            pltpu.VMEM((2, n_exp, slots, width), BF16),
            pltpu.VMEM((2, n_exp, slots, width), BF16),
            pltpu.VMEM((2, n_exp, tokens, width), BF16),
            pltpu.VMEM((2, n_exp, tokens, width), BF16),
            pltpu.VMEM((groups, 16, tokens), F32),
            pltpu.SemaphoreType.DMA((2, 2, n_exp)),
            pltpu.SemaphoreType.DMA((2, 2, n_exp, n_ctx)),
            pltpu.SemaphoreType.DMA((2, 2, n_exp)),
            pltpu.SemaphoreType.DMA((2, groups)),
        ],
        3,
        (place, slot_weight, both_grad, gate_up, hidden, down, pre_norm),
    )


def per_device(
    queries,
    latent,
    frames,
    w_uv,
    w_out,
    residual,
    norm_gain,
    expert_ids,
    mix_codes,
    w_gate,
    w_up,
    w_down,
    grad_out,
):
    ctx_count = lax.axis_size("ctx")
    ctx_place = lax.axis_index("ctx")
    group_place = lax.axis_index(GROUP)
    token_count = queries.shape[0]
    head_count, latent_width, value_width = w_uv.shape
    slice_width = residual.shape[1]
    model_width = norm_gain.shape[0]
    hidden_width = w_gate.shape[2]
    top_count = expert_ids.shape[1]
    capacity = token_count * top_count // ctx_count * 5 // 4
    slot_total = ctx_count * capacity
    sizes = (ctx_count, lax.axis_size("role"), lax.axis_size("exp"))
    paired = capacity % 16 == 0 and 2 * ctx_count == sizes[1] * sizes[2] and sizes[1] == 2

    expert_range = jnp.arange(ctx_count, dtype=jnp.int32)
    hits = expert_ids[:, :, None] == expert_range[None, None, :]
    hit = jnp.any(hits, axis=1).astype(F32)
    rows = jnp.arange(token_count, dtype=jnp.int32)
    before = (rows[None, :] < rows[:, None]).astype(BF16)
    rank = mm(hit.astype(BF16).T, before, ((1,), (1,)))
    code_values = mix_codes.astype(F32)
    mix_weight = code_values / jnp.sum(code_values, axis=1, keepdims=True)
    pair_weight = jnp.sum(jnp.where(hits, mix_weight[:, :, None], 0.0), axis=1)
    slot_range = jnp.arange(capacity, dtype=jnp.int32).astype(F32)
    place = (rank[:, None, :] == slot_range[None, :, None]) & (hit.T[:, None, :] > 0)
    slot_weight = jnp.sum(jnp.where(place, pair_weight.T[:, None, :], 0.0), axis=2).reshape(
        slot_total, 1
    )
    place = place.astype(BF16).reshape(slot_total, token_count)

    def to_experts(slot_rows):
        outgoing = slot_rows.astype(BF16).reshape(ctx_count, capacity, slice_width)
        return group_gather(context_swap(outgoing).reshape(slot_total, slice_width))

    def from_experts(partial_rows):
        summed = group_sum(partial_rows.astype(BF16))
        return context_swap(summed.reshape(ctx_count, capacity, slice_width)).reshape(
            slot_total, slice_width
        )

    down_weight = w_down[0]
    gate_up = (
        jnp.concatenate([w_gate[0], w_up[0]], axis=1).astype(F32) * norm_gain[:, None]
    ).astype(BF16)

    key_rows = lax.all_gather(latent, "ctx", axis=0, tiled=True)
    own_frames = lax.dynamic_slice_in_dim(frames, ctx_place * token_count, token_count)
    visible = frames[None, :] <= own_frames[:, None]
    query_heads = queries.reshape(token_count, head_count, latent_width)
    scores = jnp.einsum(
        "thd,sd->hts", query_heads, key_rows, preferred_element_type=F32
    ) * latent_width ** (-0.5)
    scores = jnp.where(visible[None, :, :], scores, -1e30)
    row_top = jnp.max(scores, axis=-1, keepdims=True)
    exp_scores = jnp.exp(scores - row_top)
    attn_weights = (exp_scores / jnp.sum(exp_scores, axis=-1, keepdims=True)).astype(BF16)
    latent_mix = jnp.einsum(
        "hts,sd->thd", attn_weights, key_rows, preferred_element_type=F32
    ).astype(BF16)
    head_out = jnp.einsum(
        "thd,hdv->thv", latent_mix, w_uv, preferred_element_type=F32
    ).astype(BF16)
    head_out = head_out.reshape(token_count, head_count * value_width)
    if paired:
        attn_sum, out_grad = project_out(head_out, w_out, place, slot_weight, grad_out, sizes)
        attn_sum = attn_sum.astype(F32)
    else:
        out_grad = to_experts(mm(place, grad_out, ((1,), (0,))) * slot_weight)
        column_part = jnp.dot(
            lax.all_gather(head_out, "ctx", axis=0, tiled=True), w_out, preferred_element_type=F32
        ).astype(BF16)
        column_width = column_part.shape[1]
        row_blocks = context_swap(column_part.reshape(ctx_count, token_count, column_width))
        row_part = jnp.transpose(row_blocks, (1, 0, 2)).reshape(token_count, ctx_count * column_width)
        attn_sum = group_sum(row_part).astype(F32)
    pre_norm = (residual.astype(F32) + attn_sum).astype(BF16)
    pre_wide = pre_norm.astype(F32)
    if paired:
        pre_rows = dispatch(place, pre_norm, sizes)
    else:
        pre_rows = to_experts(mm(place, pre_norm, ((1,), (0,))))
    hidden_grad = mm(out_grad, down_weight, ((1,), (1,)))
    rows_wide = pre_rows.astype(F32)
    row_inv = lax.rsqrt(jnp.mean(rows_wide * rows_wide, axis=1, keepdims=True) + 1e-06)
    both_in = mm(pre_rows, gate_up, ((1,), (0,))) * row_inv
    gate_in = both_in[:, :hidden_width]
    up_in = both_in[:, hidden_width:]
    gate_sig = jax.nn.sigmoid(gate_in)
    gate_act = gate_in * gate_sig
    hidden = (gate_act * up_in).astype(BF16)
    gate_grad = hidden_grad * up_in * gate_sig * (1.0 + gate_in * (1.0 - gate_sig))
    up_grad = hidden_grad * gate_act
    both_grad = jnp.concatenate([gate_grad, up_grad], axis=1)
    if paired:
        scaled_grad, routed, sums = combine(
            place, slot_weight, both_grad.astype(BF16), gate_up, hidden, down_weight, pre_norm, sizes
        )
        square_sum, center_sum = sums[0][:, None], sums[8][:, None]
    else:
        row_part = mm(both_grad.astype(BF16), gate_up, ((1,), (1,))).astype(BF16)
        down_part = mm(hidden, down_weight, ((1,), (0,))).astype(BF16)
        scaled_grad = mm(place, from_experts(row_part), ((0,), (0,)))
        down_back = from_experts(down_part).astype(F32) * slot_weight
        routed = mm(place, down_back.astype(BF16), ((0,), (0,)))
        square_sum = lax.psum(jnp.sum(pre_wide * pre_wide, axis=1, keepdims=True), GROUP)
        center_sum = lax.psum(jnp.sum(scaled_grad * pre_wide, axis=1, keepdims=True), GROUP)
    inv_scale = lax.rsqrt(square_sum / model_width + 1e-06)
    grad_both = mm(pre_rows, (both_grad * row_inv).astype(BF16), ((0,), (0,))) * norm_gain[:, None]
    grad_gate = grad_both[:, :hidden_width].astype(BF16)[None]
    grad_up = grad_both[:, hidden_width:].astype(BF16)[None]
    grad_down = mm(hidden, out_grad, ((0,), (0,))).astype(BF16)[None]

    center = center_sum * inv_scale / model_width
    grad_pre_norm = (
        grad_out.astype(F32) + inv_scale * (scaled_grad - pre_wide * inv_scale * center)
    ).astype(BF16)
    layer_out = (pre_wide + routed).astype(BF16)
    return (layer_out, grad_pre_norm, grad_gate, grad_up, grad_down)


def solution(mesh):
    placed = (
        P("ctx", GROUP),
        P("ctx", None),
        P(),
        P(GROUP, None, None),
        P(GROUP, "ctx"),
        P("ctx", GROUP),
        P(),
        P("ctx", None),
        P("ctx", None),
        P("ctx", None, GROUP),
        P("ctx", None, GROUP),
        P("ctx", GROUP, None),
        P("ctx", GROUP),
    )
    return jax.shard_map(
        per_device,
        mesh=mesh,
        in_specs=placed,
        out_specs=(
            P("ctx", GROUP),
            P("ctx", GROUP),
            P("ctx", None, GROUP),
            P("ctx", None, GROUP),
            P("ctx", GROUP, None),
        ),
        check_vma=False,
    )
```

```python
import jax
import jax.numpy as jnp
from jax import lax
from jax.experimental import pallas as pl
from jax.experimental.pallas import tpu as pltpu
from jax.sharding import PartitionSpec as P

GROUP = ("role", "exp")
F32 = jnp.float32
BF16 = jnp.bfloat16


def context_swap(blocks):
    return lax.all_to_all(blocks, "ctx", split_axis=0, concat_axis=0, tiled=True)


def group_sum(terms):
    return lax.psum_scatter(terms, GROUP, scatter_dimension=1, tiled=True)


def group_gather(columns):
    return lax.all_gather(columns, GROUP, axis=1, tiled=True)


def mm(a, b, dims):
    return lax.dot_general(a, b, (dims, ((), ())), preferred_element_type=F32)


def push(src, dst, send_sem, recv_sem, device):
    return pltpu.make_async_remote_copy(
        src_ref=src,
        dst_ref=dst,
        send_sem=send_sem,
        recv_sem=recv_sem,
        device_id=device,
        device_id_type=pl.DeviceIdType.MESH,
    )


def places(n_ctx, n_role, n_exp):
    c, r, z = lax.axis_index("ctx"), lax.axis_index("role"), lax.axis_index("exp")
    ctx_peers = [(lax.rem(c + k, n_ctx), r, z) for k in range(n_ctx)]
    exp_peers = [(c, r, lax.rem(z + k, n_exp)) for k in range(n_exp)]
    return c, r, z, ctx_peers, exp_peers, (c, 1 - r, z)


def greet(peers):
    barrier = pltpu.get_barrier_semaphore()
    for peer in peers:
        pl.semaphore_signal(
            barrier, inc=1, device_id=peer, device_id_type=pl.DeviceIdType.MESH
        )
    pl.semaphore_wait(barrier, len(peers))


def span(start, size):
    return pl.ds(pl.multiple_of(start * size, size), size)


def call_kernel(body, outs, scratch, number, args):
    vmem = pl.BlockSpec(memory_space=pltpu.VMEM)
    return pl.pallas_call(
        body,
        out_shape=outs,
        in_specs=[vmem] * len(args),
        out_specs=jax.tree.map(lambda _: vmem, outs),
        scratch_shapes=scratch,
        compiler_params=pltpu.CompilerParams(
            collective_id=number, has_side_effects=True, vmem_limit_bytes=58 << 20
        ),
    )(*args)


def project_out(queries, latent, visible, w_uv, w_out, place, slot_weight, block, sizes):
    n_ctx, n_role, n_exp = sizes
    tokens = latent.shape[0]
    head_count, latent_width, value_width = w_uv.shape
    depth = head_count * value_width
    width = w_out.shape[1]
    half = n_ctx * tokens // n_role
    chunk = half // n_exp
    slice_width = block.shape[1]
    slots = place.shape[0]
    cap = slots // n_ctx

    def body(
        query_ref, latent_ref, visible_ref, uv_ref, w_ref, place_ref, weight_ref, block_ref,
        out_ref, slot_ref, keys, heads, mine, theirs, parts, got, done, cols, sent,
        key_sems, sems, core_sems, exp_sems, shuffle_sems, g_sems, c_sems, p_sems,
    ):
        c, r, z, ctx_peers, exp_peers, partner = places(*sizes)
        g = r * n_exp + z
        away = c != g // 2
        owners = []
        for k in range(2):
            to = 2 * c + lax.rem(g + k, 2)
            owners.append((g // 2, to // n_exp, lax.rem(to, n_exp)))
        barrier = pltpu.get_barrier_semaphore()
        for peer in ctx_peers[1:] + exp_peers[1:] + [partner, owners[1]]:
            pl.semaphore_signal(
                barrier, inc=1, device_id=peer, device_id_type=pl.DeviceIdType.MESH
            )

        @pl.when(away)
        def _():
            pl.semaphore_signal(
                barrier, inc=1, device_id=owners[0], device_id_type=pl.DeviceIdType.MESH
            )

        pl.semaphore_wait(barrier, n_ctx + n_exp + jnp.where(away, 1, 0))
        copies = [
            push(latent_ref, keys.at[c], key_sems.at[0, k], key_sems.at[1, k], ctx_peers[k])
            for k in range(1, n_ctx)
        ]
        for copy in copies:
            copy.start()
        gathers = [None] + [
            push(block_ref, cols.at[z], g_sems.at[0, k], g_sems.at[1, k], exp_peers[k])
            for k in range(1, n_exp)
        ]
        for copy in gathers[1:]:
            copy.start()
        keys[c] = latent_ref[...]
        cols[z] = block_ref[...]
        swaps = []

        def scatter(s):
            piece = lax.rem(z + s, n_exp)
            if s:
                gathers[n_exp - s].wait_recv()
            where = span(r * n_exp + piece, slice_width)
            rows = mm(place_ref[...], cols[piece], ((1,), (0,))) * weight_ref[...]
            sent[s] = rows.astype(BF16)
            for k in range(1, n_ctx):
                copy = push(
                    sent.at[s, span(lax.rem(c + k, n_ctx), cap), :],
                    slot_ref.at[span(c, cap), where],
                    c_sems.at[0, s, k],
                    c_sems.at[1, s, k],
                    ctx_peers[k],
                )
                copy.start()
                swaps.append(copy)
            slot_ref[span(c, cap), where] = sent[s, span(c, cap), :]

        for copy in copies:
            copy.wait()
        scatter(0)
        rows = keys[...].reshape(n_ctx * tokens, latent_width)
        for h in range(head_count):
            query = query_ref[:, pl.ds(h * latent_width, latent_width)]
            scores = mm(query, rows, ((1,), (1,))) * latent_width ** (-0.5)
            scores = jnp.where(visible_ref[...] > 0, scores, -1e30)
            exps = jnp.exp(scores - jnp.max(scores, axis=1, keepdims=True))
            weights = (exps / jnp.sum(exps, axis=1, keepdims=True)).astype(BF16)
            mix = mm(weights, rows, ((1,), (0,))).astype(BF16)
            heads[c, :, pl.ds(h * value_width, value_width)] = mm(
                mix, uv_ref[h], ((1,), (0,))
            ).astype(BF16)
        copies = [
            push(heads.at[c], heads.at[c], sems.at[0, k], sems.at[1, k], ctx_peers[k])
            for k in range(1, n_ctx)
        ]
        for copy in copies:
            copy.start()
        for copy in copies:
            copy.wait()
        per_role = n_ctx // n_role
        for j in range(per_role):
            mine[pl.ds(j * tokens, tokens), :] = mm(
                heads[(1 - r) * per_role + j], w_ref[...], ((1,), (0,))
            ).astype(BF16)
        swap = push(mine, theirs, core_sems.at[0], core_sems.at[1], partner)
        swap.start()
        for j in range(per_role):
            parts[pl.ds(j * tokens, tokens), :] = mm(
                heads[r * per_role + j], w_ref[...], ((1,), (0,))
            ).astype(BF16)
        for s in range(1, n_exp):
            scatter(s)
        swap.wait()
        parts[...] = (parts[...].astype(F32) + theirs[...].astype(F32)).astype(BF16)
        copies = []
        for k in range(1, n_exp):
            target = lax.rem(z + k, n_exp)
            copy = push(
                parts.at[span(target, chunk), :],
                got.at[k],
                exp_sems.at[0, k],
                exp_sems.at[1, k],
                exp_peers[k],
            )
            copy.start()
            copies.append(copy)
        for copy in copies:
            copy.wait()
        total = parts[span(z, chunk), :].astype(F32)
        for k in range(1, n_exp):
            total = total + got[k].astype(F32)
        done[...] = total.astype(BF16)
        shuffles = []
        for k in range(2):
            shuffles.append(
                push(
                    done.at[:, span(lax.rem(g + k, 2), slice_width)],
                    out_ref.at[span(lax.rem(g, 2), chunk), :],
                    shuffle_sems.at[0, k],
                    shuffle_sems.at[1, k],
                    owners[k],
                )
            )
        shuffles[1].start()

        @pl.when(away)
        def _():
            shuffles[0].start()

        @pl.when(jnp.logical_not(away))
        def _():
            out_ref[span(lax.rem(g, 2), chunk), :] = done[:, span(lax.rem(g, 2), slice_width)]

        moves = []
        for s in range(n_exp):
            where = span(r * n_exp + lax.rem(z + s, n_exp), slice_width)
            for k in range(n_ctx):
                if k:
                    swaps[s * (n_ctx - 1) + k - 1].wait_recv()
                region = slot_ref.at[span(lax.rem(c + n_ctx - k, n_ctx), cap), where]
                move = push(region, region, p_sems.at[0, s, k], p_sems.at[1, s, k], partner)
                move.start()
                moves.append(move)
        for copy in gathers[1:] + swaps:
            copy.wait_send()
        for move in moves:
            move.wait()
        shuffles[1].wait()

        @pl.when(away)
        def _():
            shuffles[0].wait()

    return call_kernel(
        body,
        (
            jax.ShapeDtypeStruct((tokens, slice_width), BF16),
            jax.ShapeDtypeStruct((slots, slice_width * n_role * n_exp), BF16),
        ),
        [
            pltpu.VMEM((n_ctx, tokens, latent_width), BF16),
            pltpu.VMEM((n_ctx, tokens, depth), BF16),
            pltpu.VMEM((half, width), BF16),
            pltpu.VMEM((half, width), BF16),
            pltpu.VMEM((half, width), BF16),
            pltpu.VMEM((n_exp, chunk, width), BF16),
            pltpu.VMEM((chunk, width), BF16),
            pltpu.VMEM((n_exp, tokens, slice_width), BF16),
            pltpu.VMEM((n_exp, slots, slice_width), BF16),
            pltpu.SemaphoreType.DMA((2, n_ctx)),
            pltpu.SemaphoreType.DMA((2, n_ctx)),
            pltpu.SemaphoreType.DMA((2,)),
            pltpu.SemaphoreType.DMA((2, n_exp)),
            pltpu.SemaphoreType.DMA((2, 2)),
            pltpu.SemaphoreType.DMA((2, n_exp)),
            pltpu.SemaphoreType.DMA((2, n_exp, n_ctx)),
            pltpu.SemaphoreType.DMA((2, n_exp, n_ctx)),
        ],
        1,
        (queries, latent, visible, w_uv, w_out, place, slot_weight, block),
    )


def dispatch(place, block, sizes):
    n_ctx, n_role, n_exp = sizes
    tokens, width = block.shape
    slots = place.shape[0]
    cap = slots // n_ctx
    half = width * n_exp

    def body(place_ref, block_ref, out_ref, cols, sent, z_sems, c_sems, p_sems):
        c, r, z, ctx_peers, exp_peers, partner = places(*sizes)
        greet(ctx_peers[1:] + exp_peers[1:] + [partner])
        gathers = [None] + [
            push(block_ref, cols.at[z], z_sems.at[0, k], z_sems.at[1, k], exp_peers[k])
            for k in range(1, n_exp)
        ]
        for copy in gathers[1:]:
            copy.start()
        cols[z] = block_ref[...]
        swaps = []
        for s in range(n_exp):
            piece = lax.rem(z + s, n_exp)
            if s:
                gathers[n_exp - s].wait_recv()
            where = span(r * n_exp + piece, width)
            sent[s] = mm(place_ref[...], cols[piece], ((1,), (0,))).astype(BF16)
            for k in range(1, n_ctx):
                target = lax.rem(c + k, n_ctx)
                copy = push(
                    sent.at[s, span(target, cap), :],
                    out_ref.at[span(c, cap), where],
                    c_sems.at[0, s, k],
                    c_sems.at[1, s, k],
                    ctx_peers[k],
                )
                copy.start()
                swaps.append((s, k, where, copy))
            out_ref[span(c, cap), where] = sent[s, span(c, cap), :]
        moves = []
        for s in range(n_exp):
            where = span(r * n_exp + lax.rem(z + s, n_exp), width)
            for k in range(n_ctx):
                if k:
                    swaps[s * (n_ctx - 1) + k - 1][3].wait_recv()
                region = out_ref.at[span(lax.rem(c + n_ctx - k, n_ctx), cap), where]
                move = push(region, region, p_sems.at[0, s, k], p_sems.at[1, s, k], partner)
                move.start()
                moves.append(move)
        for copy in gathers[1:]:
            copy.wait_send()
        for item in swaps:
            item[3].wait_send()
        for move in moves:
            move.wait()

    return call_kernel(
        body,
        jax.ShapeDtypeStruct((slots, half * n_role), BF16),
        [
            pltpu.VMEM((n_exp, tokens, width), BF16),
            pltpu.VMEM((n_exp, slots, width), BF16),
            pltpu.SemaphoreType.DMA((2, n_exp)),
            pltpu.SemaphoreType.DMA((2, n_exp, n_ctx)),
            pltpu.SemaphoreType.DMA((2, n_exp, n_ctx)),
        ],
        2,
        (place, block),
    )


def combine(place, slot_weight, both_grad, gate_up, hidden, down, pre_norm, sizes):
    n_ctx, n_role, n_exp = sizes
    slots, tokens = place.shape
    cap = slots // n_ctx
    width = pre_norm.shape[1]
    groups = n_role * n_exp

    def body(
        place_ref, weight_ref, both_ref, wide_ref, hidden_ref, down_ref, pre_ref,
        row_out, down_out, sum_out, mine, theirs, sent, got, back, last, sums,
        p_sems, c_sems, z_sems, s_sems,
    ):
        c, r, z, ctx_peers, exp_peers, partner = places(*sizes)
        group_peers = [
            (c, lax.rem(r + k // n_exp, n_role), lax.rem(z + k, n_exp)) for k in range(groups)
        ]
        greet(ctx_peers[1:] + group_peers[1:])
        order = [(i, s) for i in range(2) for s in list(range(1, n_exp)) + [0]]
        firsts, swaps, finals = {}, {}, []

        def product(i, role, piece):
            where = span(role * n_exp + piece, width)
            if i == 0:
                return mm(both_ref[...], wide_ref[where, :], ((1,), (1,)))
            return mm(hidden_ref[...], down_ref[:, where], ((1,), (0,)))

        def offer(i, s):
            mine[i, s] = product(i, 1 - r, lax.rem(z + s, n_exp)).astype(BF16)
            firsts[i, s] = push(
                mine.at[i, s], theirs.at[i, s], p_sems.at[0, i, s], p_sems.at[1, i, s], partner
            )
            firsts[i, s].start()

        offer(*order[0])
        for at, (i, s) in enumerate(order):
            if at + 1 < len(order):
                offer(*order[at + 1])
            own = product(i, r, lax.rem(z + s, n_exp))
            firsts[i, s].wait_recv()
            sent[i, s] = (own + theirs[i, s].astype(F32)).astype(BF16)
            for k in range(1, n_ctx):
                copy = push(
                    sent.at[i, s, span(lax.rem(c + k, n_ctx), cap), :],
                    got.at[i, s, span(c, cap), :],
                    c_sems.at[0, i, s, k],
                    c_sems.at[1, i, s, k],
                    ctx_peers[k],
                )
                copy.start()
                swaps[i, s, k] = copy
            got[i, s, span(c, cap), :] = sent[i, s, span(c, cap), :]
        for i, s in order:
            for k in range(1, n_ctx):
                swaps[i, s, k].wait_recv()
            rows = got[i, s]
            if i == 1:
                rows = (rows.astype(F32) * weight_ref[...]).astype(BF16)
            merged = mm(place_ref[...], rows, ((0,), (0,)))
            if s == 0:
                (row_out, down_out)[i][...] = merged
            else:
                back[i, s] = merged.astype(BF16)
                copy = push(
                    back.at[i, s],
                    last.at[i, s],
                    z_sems.at[0, i, s],
                    z_sems.at[1, i, s],
                    exp_peers[s],
                )
                copy.start()
                finals.append((i, s, copy))
        def take(item):
            for i, s, copy in finals:
                if i == item:
                    copy.wait_recv()
                    target = (row_out, down_out)[i]
                    target[...] = target[...] + last[i, s].astype(F32)

        def row_sums(values):
            return lax.dot_general(
                jnp.ones((8, width), F32),
                values,
                (((1,), (1,)), ((), ())),
                precision=lax.Precision.HIGHEST,
                preferred_element_type=F32,
            )

        take(0)
        pre = pre_ref[...].astype(F32)
        sums[0, pl.ds(0, 8), :] = row_sums(pre * pre)
        sums[0, pl.ds(8, 8), :] = row_sums(pre * row_out[...])
        shares = []
        for k in range(1, groups):
            copy = push(sums.at[0], sums.at[k], s_sems.at[0, k], s_sems.at[1, k], group_peers[k])
            copy.start()
            shares.append(copy)
        take(1)
        total = sums[0]
        for k in range(1, groups):
            shares[k - 1].wait_recv()
            total = total + sums[k]
        sum_out[...] = total
        for copy in list(firsts.values()) + list(swaps.values()) + [f[2] for f in finals]:
            copy.wait_send()
        for copy in shares:
            copy.wait_send()

    out = jax.ShapeDtypeStruct((tokens, width), F32)
    return call_kernel(
        body,
        (out, out, jax.ShapeDtypeStruct((16, tokens), F32)),
        [
            pltpu.VMEM((2, n_exp, slots, width), BF16),
            pltpu.VMEM((2, n_exp, slots, width), BF16),
            pltpu.VMEM((2, n_exp, slots, width), BF16),
            pltpu.VMEM((2, n_exp, slots, width), BF16),
            pltpu.VMEM((2, n_exp, tokens, width), BF16),
            pltpu.VMEM((2, n_exp, tokens, width), BF16),
            pltpu.VMEM((groups, 16, tokens), F32),
            pltpu.SemaphoreType.DMA((2, 2, n_exp)),
            pltpu.SemaphoreType.DMA((2, 2, n_exp, n_ctx)),
            pltpu.SemaphoreType.DMA((2, 2, n_exp)),
            pltpu.SemaphoreType.DMA((2, groups)),
        ],
        3,
        (place, slot_weight, both_grad, gate_up, hidden, down, pre_norm),
    )


def per_device(
    queries,
    latent,
    frames,
    w_uv,
    w_out,
    residual,
    norm_gain,
    expert_ids,
    mix_codes,
    w_gate,
    w_up,
    w_down,
    grad_out,
):
    ctx_count = lax.axis_size("ctx")
    ctx_place = lax.axis_index("ctx")
    group_place = lax.axis_index(GROUP)
    token_count = queries.shape[0]
    head_count, latent_width, value_width = w_uv.shape
    slice_width = residual.shape[1]
    model_width = norm_gain.shape[0]
    hidden_width = w_gate.shape[2]
    top_count = expert_ids.shape[1]
    capacity = token_count * top_count // ctx_count * 5 // 4
    slot_total = ctx_count * capacity
    sizes = (ctx_count, lax.axis_size("role"), lax.axis_size("exp"))
    paired = capacity % 16 == 0 and 2 * ctx_count == sizes[1] * sizes[2] and sizes[1] == 2

    expert_range = jnp.arange(ctx_count, dtype=jnp.int32)
    hits = expert_ids[:, :, None] == expert_range[None, None, :]
    hit = jnp.any(hits, axis=1).astype(F32)
    rows = jnp.arange(token_count, dtype=jnp.int32)
    before = (rows[None, :] < rows[:, None]).astype(BF16)
    rank = mm(hit.astype(BF16).T, before, ((1,), (1,)))
    code_values = mix_codes.astype(F32)
    mix_weight = code_values / jnp.sum(code_values, axis=1, keepdims=True)
    pair_weight = jnp.sum(jnp.where(hits, mix_weight[:, :, None], 0.0), axis=1)
    slot_range = jnp.arange(capacity, dtype=jnp.int32).astype(F32)
    place = (rank[:, None, :] == slot_range[None, :, None]) & (hit.T[:, None, :] > 0)
    slot_weight = jnp.sum(jnp.where(place, pair_weight.T[:, None, :], 0.0), axis=2).reshape(
        slot_total, 1
    )
    place = place.astype(BF16).reshape(slot_total, token_count)

    def to_experts(slot_rows):
        outgoing = slot_rows.astype(BF16).reshape(ctx_count, capacity, slice_width)
        return group_gather(context_swap(outgoing).reshape(slot_total, slice_width))

    def from_experts(partial_rows):
        summed = group_sum(partial_rows.astype(BF16))
        return context_swap(summed.reshape(ctx_count, capacity, slice_width)).reshape(
            slot_total, slice_width
        )

    down_weight = w_down[0]
    gate_up = (
        jnp.concatenate([w_gate[0], w_up[0]], axis=1).astype(F32) * norm_gain[:, None]
    ).astype(BF16)

    own_frames = lax.dynamic_slice_in_dim(frames, ctx_place * token_count, token_count)
    visible = frames[None, :] <= own_frames[:, None]
    if paired:
        attn_sum, out_grad = project_out(
            queries, latent, visible.astype(F32), w_uv, w_out, place, slot_weight, grad_out, sizes
        )
        attn_sum = attn_sum.astype(F32)
    else:
        key_rows = lax.all_gather(latent, "ctx", axis=0, tiled=True)
        query_heads = queries.reshape(token_count, head_count, latent_width)
        scores = jnp.einsum(
            "thd,sd->hts", query_heads, key_rows, preferred_element_type=F32
        ) * latent_width ** (-0.5)
        scores = jnp.where(visible[None, :, :], scores, -1e30)
        row_top = jnp.max(scores, axis=-1, keepdims=True)
        exp_scores = jnp.exp(scores - row_top)
        attn_weights = (exp_scores / jnp.sum(exp_scores, axis=-1, keepdims=True)).astype(BF16)
        latent_mix = jnp.einsum(
            "hts,sd->thd", attn_weights, key_rows, preferred_element_type=F32
        ).astype(BF16)
        head_out = jnp.einsum(
            "thd,hdv->thv", latent_mix, w_uv, preferred_element_type=F32
        ).astype(BF16)
        head_out = head_out.reshape(token_count, head_count * value_width)
        out_grad = to_experts(mm(place, grad_out, ((1,), (0,))) * slot_weight)
        column_part = jnp.dot(
            lax.all_gather(head_out, "ctx", axis=0, tiled=True), w_out, preferred_element_type=F32
        ).astype(BF16)
        column_width = column_part.shape[1]
        row_blocks = context_swap(column_part.reshape(ctx_count, token_count, column_width))
        row_part = jnp.transpose(row_blocks, (1, 0, 2)).reshape(token_count, ctx_count * column_width)
        attn_sum = group_sum(row_part).astype(F32)
    pre_norm = (residual.astype(F32) + attn_sum).astype(BF16)
    pre_wide = pre_norm.astype(F32)
    if paired:
        pre_rows = dispatch(place, pre_norm, sizes)
    else:
        pre_rows = to_experts(mm(place, pre_norm, ((1,), (0,))))
    hidden_grad = mm(out_grad, down_weight, ((1,), (1,)))
    rows_wide = pre_rows.astype(F32)
    row_inv = lax.rsqrt(jnp.mean(rows_wide * rows_wide, axis=1, keepdims=True) + 1e-06)
    both_in = mm(pre_rows, gate_up, ((1,), (0,))) * row_inv
    gate_in = both_in[:, :hidden_width]
    up_in = both_in[:, hidden_width:]
    gate_sig = jax.nn.sigmoid(gate_in)
    gate_act = gate_in * gate_sig
    hidden = (gate_act * up_in).astype(BF16)
    gate_grad = hidden_grad * up_in * gate_sig * (1.0 + gate_in * (1.0 - gate_sig))
    up_grad = hidden_grad * gate_act
    both_grad = jnp.concatenate([gate_grad, up_grad], axis=1)
    if paired:
        scaled_grad, routed, sums = combine(
            place, slot_weight, both_grad.astype(BF16), gate_up, hidden, down_weight, pre_norm, sizes
        )
        square_sum, center_sum = sums[0][:, None], sums[8][:, None]
    else:
        row_part = mm(both_grad.astype(BF16), gate_up, ((1,), (1,))).astype(BF16)
        down_part = mm(hidden, down_weight, ((1,), (0,))).astype(BF16)
        scaled_grad = mm(place, from_experts(row_part), ((0,), (0,)))
        down_back = from_experts(down_part).astype(F32) * slot_weight
        routed = mm(place, down_back.astype(BF16), ((0,), (0,)))
        square_sum = lax.psum(jnp.sum(pre_wide * pre_wide, axis=1, keepdims=True), GROUP)
        center_sum = lax.psum(jnp.sum(scaled_grad * pre_wide, axis=1, keepdims=True), GROUP)
    inv_scale = lax.rsqrt(square_sum / model_width + 1e-06)
    grad_both = mm(pre_rows, (both_grad * row_inv).astype(BF16), ((0,), (0,))) * norm_gain[:, None]
    grad_gate = grad_both[:, :hidden_width].astype(BF16)[None]
    grad_up = grad_both[:, hidden_width:].astype(BF16)[None]
    grad_down = mm(hidden, out_grad, ((0,), (0,))).astype(BF16)[None]

    center = center_sum * inv_scale / model_width
    grad_pre_norm = (
        grad_out.astype(F32) + inv_scale * (scaled_grad - pre_wide * inv_scale * center)
    ).astype(BF16)
    layer_out = (pre_wide + routed).astype(BF16)
    return (layer_out, grad_pre_norm, grad_gate, grad_up, grad_down)


def solution(mesh):
    placed = (
        P("ctx", GROUP),
        P("ctx", None),
        P(),
        P(GROUP, None, None),
        P(GROUP, "ctx"),
        P("ctx", GROUP),
        P(),
        P("ctx", None),
        P("ctx", None),
        P("ctx", None, GROUP),
        P("ctx", None, GROUP),
        P("ctx", GROUP, None),
        P("ctx", GROUP),
    )
    return jax.shard_map(
        per_device,
        mesh=mesh,
        in_specs=placed,
        out_specs=(
            P("ctx", GROUP),
            P("ctx", GROUP),
            P("ctx", None, GROUP),
            P("ctx", None, GROUP),
            P("ctx", GROUP, None),
        ),
        check_vma=False,
    )
```
